32 devices in a mesh: guide: 2 (over core), blk: 4 (over z), batch: 4 (over y, x).
Axes of the slice: x: 2, y: 2, z: 4, core: 2. Of those that a mesh axis runs over, the one named last changes fastest.
Arguments:
- hidden: bfloat16 [2, 64, 1536], P('guide', 'batch'), may hold values from -6 to 6
- w_qkv: bfloat16 [1536, 2560], P('blk'), may hold values from -0.15625 to 0.15625
- key_cache: bfloat16 [2, 64, 64, 512], P('guide', 'batch', 'blk'), may hold values from -700 to 700
- value_cache: bfloat16 [2, 64, 64, 512], P('guide', 'batch', 'blk'), may hold values from -6 to 6
- lengths: int32 [2, 64], P('guide', 'batch'), may hold values from 8 to 64, as said below
- w_out: bfloat16 [1536, 1536], P('blk'), may hold values from -0.15625 to 0.15625
- router: bfloat16 [1536, 16], replicated, may hold values from -0.15625 to 0.15625
- routes: int32 [2, 64, 2], P('guide', 'batch'), may hold values from 0 to 15, all different within a row
- w_gate: bfloat16 [1536, 16384], P(None, 'blk'), may hold values from -0.15625 to 0.15625
- w_up: bfloat16 [1536, 16384], P(None, 'blk'), may hold values from -0.15625 to 0.15625
- w_down: bfloat16 [16384, 1536], P('blk'), may hold values from -0.125 to 0.125
- w_vocab: bfloat16 [1536, 65536], P(None, ('blk', 'batch')), may hold values from -0.15625 to 0.15625
- group_ids: int32 [64], replicated, may hold values from 0 to 7, never falling along the last dimension, each value on 1 to 16 neighbouring positions
- weight_index: int32 [8], replicated, may hold values from 0 to 7
- guidance_levels: float32 [8], replicated, may hold values from 1 to 5
Outputs:
- logits: float32 [64, 65536], P('guide', ('blk', 'batch'))
- new_keys: bfloat16 [2, 64, 512], P('guide', 'batch')
- new_values: bfloat16 [2, 64, 512], P('guide', 'batch')
The draws below stay inside these ranges and needn't reach their ends.
Inputs may be any that keep to these rules, and one draw needn't show every extreme that they name: `lengths`: every stream and index of batch has a request whose cache is full.
All inputs are finite; a program needn't handle non-finite values.
Results may differ from the reference program's by a relative error of at most 0.008.
Values may be sent and summed in bfloat16 or wider, within the bound.
A program may use at most 128 MiB of HBM per device.

```python
import math
import jax
import jax.numpy as jnp
import numpy as np
from jax import lax

D = 1536
HEADS = 24
KV_HEADS = 8
HEAD_DIM = 64
EXPERTS = 16
EXPERT_UNITS = 1024
VOCAB = 65536
REQ_DEV = 16
LEVELS = 8
REQUESTS = 64
GROUPS = 8
CACHE = 64


def draw_lengths(key, part):
    drawn = jax.random.randint(key, (2, REQUESTS), CACHE // 8, CACHE + 1)
    column = jnp.arange(REQUESTS)[None, :]
    block_start = column % REQ_DEV == 0
    return jnp.where(block_start, CACHE, drawn).astype(jnp.int32)


def draw_key_cache(key, part):
    key_base = jax.random.fold_in(key, 0)
    shape = (2, REQUESTS, CACHE, KV_HEADS * HEAD_DIM)
    base = jnp.clip(jax.random.normal(key_base, shape, jnp.float32), -4.0, 4.0)
    return base.astype(jnp.bfloat16)


def with_ends(entries, rng, low, high):
    longest = entries.shape.index(max(entries.shape))
    spots = []
    for shift in (0, 1):
        where = [jax.random.randint(jax.random.fold_in(rng, axis), (), 0, length) for axis, length in enumerate(entries.shape)]
        where[longest] = (where[longest] + shift) % entries.shape[longest]
        spots.append(tuple(where))
    return entries.at[spots[0]].set(low).at[spots[1]].set(high)


def block_levels(own_key, dims, cuts, smallest, high):
    loudness = 1.0
    for dim, blocks in cuts:
        steps = jax.random.uniform(jax.random.fold_in(jax.random.fold_in(own_key, 6), dim), (blocks,), jnp.float32, smallest / len(cuts), high / len(cuts))
        loudness = loudness * jnp.repeat(jnp.exp(steps), dims[dim] // blocks).reshape((-1,) + (1,) * (len(dims) - 1 - dim))
    return loudness


def choose_distinct(rng, rows, number_of, top, lift):
    order = jax.random.permutation(jax.random.fold_in(rng, 1), number_of)
    boost = order
    for power in range(3):
        boost = boost * boost // number_of
    boost = boost * lift // number_of
    lots = jax.random.randint(jax.random.fold_in(rng, 2), (rows, number_of), 0, 4096) + boost
    holders = jax.random.permutation(jax.random.fold_in(rng, 3), rows)[jnp.arange(number_of) % rows]
    lots = jnp.where(jnp.arange(rows)[:, None] == holders[None, :], 1 << 14, lots)
    priority = lots * number_of + jnp.arange(number_of)
    return lax.top_k(priority.astype(jnp.int32), top)[1].astype(jnp.int32)


def split_up(number_of, total, bound, skew):
    loads = [(1 << 20) // math.isqrt(grade ** skew) + 1 for grade in range(2, number_of + 1)]
    spare, holding = total - bound - (number_of - 1), [1] * (number_of - 1)
    while spare > 0:
        free = [i for i in range(number_of - 1) if holding[i] < bound]
        whole, budget = sum([loads[i] for i in free]), spare
        for i in free:
            extra = min(bound - holding[i], max(1, budget * loads[i] // whole), spare)
            holding[i] = holding[i] + extra
            spare = spare - extra
    return np.array([bound] + holding)


def ragged_sizes(rng, count, total, reach, lean):
    if count == 2:
        one = jax.random.randint(rng, (), max(1, total - reach), min(reach, total - 1) + 1)
        return jnp.stack([one, total - one])
    tallies = jnp.asarray(split_up(count, total, reach, lean), jnp.int32)
    couples = (count - 1) // 2
    giver, receiver = tallies[1:1 + 2 * couples:2], tallies[2:2 + 2 * couples:2]
    margin = jnp.minimum(giver - 1, reach - receiver)
    moved = jax.random.randint(jax.random.fold_in(rng, 1), (couples,), 0, 1 << 20) % (margin + 1)
    tallies = tallies.at[1:1 + 2 * couples:2].set(giver - moved).at[2:2 + 2 * couples:2].set(receiver + moved)
    return tallies[jax.random.permutation(jax.random.fold_in(rng, 2), count)]


def centred(own_key, dims, width, reach, shards=(), held_as=jnp.bfloat16):
    entries = jax.random.normal(own_key, dims, jnp.float32) * width
    if len(shards) > 0:
        entries = block_levels(own_key, dims, shards, -0.22, 0.18) * entries
    return jnp.clip(entries, min=-reach, max=reach).astype(held_as)


def setup_inputs(seed: int = 0) -> dict:
    key_list = jax.random.split(jax.random.key(seed), 16)
    hidden = centred(key_list[0], (2, REQUESTS, D), 1.0, 6.0, ((0, 2), (1, 4)))
    w_qkv = centred(key_list[1], (D, (HEADS + 2 * KV_HEADS) * HEAD_DIM), D ** -0.5, 0.15625, ((0, 4),))
    key_cache = draw_key_cache(jax.random.fold_in(key_list[15], 71), 0)
    value_cache = centred(key_list[3], (2, REQUESTS, CACHE, KV_HEADS * HEAD_DIM), 1.0, 6.0, ((0, 2), (1, 4), (2, 4)))
    lengths = draw_lengths(jax.random.fold_in(key_list[15], 71), 0)
    w_out = centred(key_list[5], (HEADS * HEAD_DIM, D), (HEADS * HEAD_DIM) ** -0.5, 0.15625, ((0, 4),))
    router = centred(key_list[6], (D, EXPERTS), D ** -0.5, 0.15625)
    routes = choose_distinct(key_list[7], 2 * REQUESTS, EXPERTS, 2, 1024).reshape((2, REQUESTS, 2))
    w_gate = centred(key_list[8], (D, EXPERTS * EXPERT_UNITS), D ** -0.5, 0.15625, ((1, 4),))
    w_up = centred(key_list[9], (D, EXPERTS * EXPERT_UNITS), D ** -0.5, 0.15625, ((1, 4),))
    w_down = centred(key_list[10], (EXPERTS * EXPERT_UNITS, D), (2 * EXPERT_UNITS) ** -0.5, 0.125, ((0, 4),))
    w_vocab = centred(key_list[11], (D, VOCAB), D ** -0.5, 0.15625, ((1, 16),))
    group_ids = jnp.searchsorted(jnp.cumsum(ragged_sizes(key_list[12], GROUPS, REQUESTS, 16, 0)), jnp.arange(REQUESTS), side="right").astype(jnp.int32)
    weight_index = with_ends(jax.random.randint(key_list[13], (GROUPS,), 0, LEVELS), jax.random.fold_in(key_list[13], 1), 0, LEVELS - 1).astype(jnp.int32)
    guidance_levels = jnp.clip(jax.random.uniform(key_list[14], (LEVELS,), jnp.float32, 1.0, 5.0), 1.0, 5.0)
    return {"hidden": hidden, "w_qkv": w_qkv, "key_cache": key_cache, "value_cache": value_cache, "lengths": lengths, "w_out": w_out, "router": router, "routes": routes, "w_gate": w_gate, "w_up": w_up, "w_down": w_down, "w_vocab": w_vocab, "group_ids": group_ids, "weight_index": weight_index, "guidance_levels": guidance_levels}


EPS = 1e-05

def rms(values):
    return values * lax.rsqrt(lax.optimization_barrier(jnp.mean(values * values, axis=-1, keepdims=True)) + EPS)

def stream_pass(x_in, key_c, value_c, lens, w_qkv, w_out, router, routes_s, w_gate, w_up, w_down, w_vocab):
    width_q = HEADS * HEAD_DIM
    width_k = KV_HEADS * HEAD_DIM
    group = HEADS // KV_HEADS
    count = x_in.shape[0]
    x = x_in.astype(jnp.float32)
    normed = rms(x).astype(jnp.bfloat16)
    qkv = jnp.dot(normed, w_qkv, preferred_element_type=jnp.float32)
    query = qkv[:, :width_q].astype(jnp.bfloat16)
    new_key = qkv[:, width_q:width_q + width_k].astype(jnp.bfloat16)
    new_value = qkv[:, width_q + width_k:].astype(jnp.bfloat16)
    qf = query.astype(jnp.float32).reshape(count, KV_HEADS, group, HEAD_DIM)
    kf = key_c.astype(jnp.float32).reshape(count, CACHE, KV_HEADS, HEAD_DIM)
    vf = value_c.astype(jnp.float32).reshape(count, CACHE, KV_HEADS, HEAD_DIM)
    scale = HEAD_DIM ** (-0.5)
    scores = jnp.einsum('rkgd,rckd->rkgc', qf, kf) * scale
    own = jnp.einsum('rkgd,rkd->rkg', qf, new_key.astype(jnp.float32).reshape(count, KV_HEADS, HEAD_DIM)) * scale
    valid = (jnp.arange(CACHE)[None, :] < lens[:, None])[:, None, None, :]
    top = jnp.maximum(lax.optimization_barrier(jnp.max(jnp.where(valid, scores, -1e+30), axis=-1)), own)
    probs = jnp.exp(jnp.where(valid, scores - top[..., None], -1e+30))
    own_prob = jnp.exp(own - top)
    total = lax.optimization_barrier(jnp.sum(probs, axis=-1)) + own_prob
    probs_r = lax.optimization_barrier(probs.astype(jnp.bfloat16)).astype(jnp.float32)
    own_r = lax.optimization_barrier(own_prob.astype(jnp.bfloat16)).astype(jnp.float32)
    acc = jnp.einsum('rkgc,rckd->rkgd', probs_r, vf)
    acc = acc + own_r[..., None] * new_value.astype(jnp.float32).reshape(count, KV_HEADS, 1, HEAD_DIM)
    attn = (acc / total[..., None]).reshape(count, width_q).astype(jnp.bfloat16)
    mixed = x + jnp.dot(attn, w_out, preferred_element_type=jnp.float32)
    expert_in = rms(mixed).astype(jnp.bfloat16)
    choice_logits = jnp.dot(expert_in, router, preferred_element_type=jnp.float32)
    picks = (routes_s[:, :, None] == jnp.arange(EXPERTS)[None, None, :]).astype(jnp.float32)
    chosen = lax.optimization_barrier(jnp.sum(picks * choice_logits[:, None, :], axis=-1))
    first = jax.nn.sigmoid(chosen[:, 0] - chosen[:, 1])
    shares = jnp.stack([first, 1.0 - first], axis=1)
    per_expert = lax.optimization_barrier(jnp.sum(picks * shares[:, :, None], axis=1))
    unit_weight = jnp.repeat(per_expert, EXPERT_UNITS, axis=1)
    gate = jnp.dot(expert_in, w_gate, preferred_element_type=jnp.float32)
    upper = jnp.dot(expert_in, w_up, preferred_element_type=jnp.float32)
    act = (jax.nn.silu(gate) * upper * unit_weight).astype(jnp.bfloat16)
    outgoing = mixed + jnp.dot(act, w_down, preferred_element_type=jnp.float32)
    final_in = rms(outgoing).astype(jnp.bfloat16)
    stream_logits = jnp.dot(final_in, w_vocab, preferred_element_type=jnp.float32).astype(jnp.bfloat16)
    return (stream_logits, new_key, new_value)

def reference(hidden, w_qkv, key_cache, value_cache, lengths, w_out, router, routes, w_gate, w_up, w_down, w_vocab, group_ids, weight_index, guidance_levels):
    results = []
    for stream in range(2):
        results.append(stream_pass(hidden[stream], key_cache[stream], value_cache[stream], lengths[stream], w_qkv, w_out, router, routes[stream], w_gate, w_up, w_down, w_vocab))
    cond = results[0][0].astype(jnp.float32)
    uncond = results[1][0].astype(jnp.float32)
    member = (group_ids[:, None] == jnp.arange(GROUPS)[None, :]).astype(jnp.float32)
    level_pick = (weight_index[:, None] == jnp.arange(LEVELS)[None, :]).astype(jnp.float32)
    group_weight = lax.optimization_barrier(jnp.sum(level_pick * guidance_levels[None, :], axis=1))
    request_weight = lax.optimization_barrier(jnp.sum(member * group_weight[None, :], axis=1))
    logits = uncond + request_weight[:, None] * (cond - uncond)
    new_keys = jnp.stack([results[0][1], results[1][1]], axis=0)
    new_values = jnp.stack([results[0][2], results[1][2]], axis=0)
    return (logits, new_keys, new_values)
```

```python
import functools

import jax
import jax.numpy as jnp
from jax import lax
from jax.experimental import pallas as pl
from jax.experimental.pallas import tpu as pltpu
from jax.sharding import PartitionSpec as P

HEADS = 24
KV_HEADS = 8
HEAD_DIM = 64
EXPERTS = 16
EXPERT_UNITS = 1024


EPS = 1e-05


def from_partner(value, axis, bit):
    mask = 2**bit
    pairs = [(source, source ^ mask) for source in range(lax.axis_size(axis))]
    return lax.ppermute(value, axis, pairs)


def rms(values):
    return values * lax.rsqrt(jnp.mean(values * values, axis=-1, keepdims=True) + EPS)


def local(
    hidden,
    w_qkv,
    key_cache,
    value_cache,
    lengths,
    w_out,
    router,
    routes,
    w_gate,
    w_up,
    w_down,
    w_vocab,
    group_ids,
    weight_index,
    guidance_levels,
):
    width_q = HEADS * HEAD_DIM
    width_k = KV_HEADS * HEAD_DIM
    group = HEADS // KV_HEADS
    position_block = lax.axis_index("blk")
    count = hidden.shape[1]
    x = hidden[0].astype(jnp.float32)
    normed = rms(x).astype(jnp.bfloat16)
    feat_rows = w_qkv.shape[0]
    normed_part = lax.dynamic_slice_in_dim(normed, position_block * feat_rows, feat_rows, 1)
    partial_qkv = jnp.dot(normed_part, w_qkv, preferred_element_type=jnp.float32)
    qkv = lax.psum(partial_qkv, "blk").astype(jnp.bfloat16)
    query = qkv[:, :width_q]
    new_key = qkv[:, width_q : width_q + width_k]
    new_value = qkv[:, width_q + width_k :]
    span = key_cache.shape[2]
    query_heads = query.reshape(count, KV_HEADS, group, HEAD_DIM)
    keys_here = key_cache[0].reshape(count, span, KV_HEADS, HEAD_DIM)
    values_here = value_cache[0].reshape(count, span, KV_HEADS, HEAD_DIM)
    scale = HEAD_DIM ** (-0.5)
    scores = (
        jnp.einsum("rkgd,rckd->rkgc", query_heads, keys_here, preferred_element_type=jnp.float32)
        * scale
    )
    own = (
        jnp.einsum(
            "rkgd,rkd->rkg",
            query_heads,
            new_key.reshape(count, KV_HEADS, HEAD_DIM),
            preferred_element_type=jnp.float32,
        )
        * scale
    )
    positions = position_block * span + jnp.arange(span)
    valid = (positions[None, :] < lengths[0][:, None])[:, None, None, :]
    local_top = jnp.max(jnp.where(valid, scores, -1e30), axis=-1)
    top = lax.pmax(jnp.maximum(local_top, own), "blk")
    probs = jnp.exp(jnp.where(valid, scores - top[..., None], -1e30))
    partial_total = jnp.sum(probs, axis=-1)
    acc = jnp.einsum(
        "rkgc,rckd->rkgd",
        probs.astype(jnp.bfloat16),
        values_here,
        preferred_element_type=jnp.float32,
    ).reshape(count, width_q)
    own_prob = jnp.exp(own - top)
    own_rounded = lax.optimization_barrier(own_prob.astype(jnp.bfloat16)).astype(jnp.float32)
    own_term = (
        own_rounded[..., None] * new_value.astype(jnp.float32).reshape(count, KV_HEADS, 1, HEAD_DIM)
    ).reshape(count, width_q)
    out_rows = w_out.shape[0]
    acc_sum, total_sum = lax.psum((acc, partial_total), "blk")
    totals = jnp.repeat((total_sum + own_prob).reshape(count, HEADS), HEAD_DIM, axis=1)
    attn = ((acc_sum + own_term) / totals).astype(jnp.bfloat16)
    attn_cols = lax.dynamic_slice_in_dim(attn, position_block * out_rows, out_rows, 1)
    mixed = x + lax.psum(jnp.dot(attn_cols, w_out, preferred_element_type=jnp.float32), "blk")
    expert_in = rms(mixed).astype(jnp.bfloat16)
    choice_logits = jnp.dot(expert_in, router, preferred_element_type=jnp.float32)
    picks = (routes[0][:, :, None] == jnp.arange(EXPERTS)[None, None, :]).astype(jnp.float32)
    chosen = jnp.sum(picks * choice_logits[:, None, :], axis=-1)
    first = jax.nn.sigmoid(chosen[:, 0] - chosen[:, 1])
    shares = jnp.stack([first, 1.0 - first], axis=1)
    per_expert = jnp.sum(picks * shares[:, :, None], axis=1)
    local_units = w_gate.shape[1]
    owner = (position_block * local_units + jnp.arange(local_units)) // EXPERT_UNITS
    member = (owner[None, :] == jnp.arange(EXPERTS)[:, None]).astype(jnp.float32)
    unit_weight = jnp.sum(per_expert[:, :, None] * member[None, :, :], axis=1)
    gate = jnp.dot(expert_in, w_gate, preferred_element_type=jnp.float32)
    upper = jnp.dot(expert_in, w_up, preferred_element_type=jnp.float32)
    act = (jax.nn.silu(gate) * upper * unit_weight).astype(jnp.bfloat16)
    expert_out = lax.psum(jnp.dot(act, w_down, preferred_element_type=jnp.float32), "blk")
    final_in = rms(mixed + expert_out).astype(jnp.bfloat16)
    stream_logits = jnp.dot(
        lax.all_gather(final_in, "batch", axis=0, tiled=True),
        w_vocab,
        preferred_element_type=jnp.float32,
    ).astype(jnp.bfloat16)
    stream_index = lax.axis_index("guide")
    half_rows = stream_logits.shape[0] // 2
    kept_rows = lax.dynamic_slice_in_dim(stream_logits, stream_index * half_rows, half_rows, 0)
    sent_rows = lax.dynamic_slice_in_dim(
        stream_logits, (1 - stream_index) * half_rows, half_rows, 0
    )
    partner = from_partner(sent_rows, "guide", 0)
    is_first = stream_index == 0
    cond = jnp.where(is_first, kept_rows, partner).astype(jnp.float32)
    uncond = jnp.where(is_first, partner, kept_rows).astype(jnp.float32)
    group_count = weight_index.shape[0]
    level_count = guidance_levels.shape[0]
    in_group = (group_ids[:, None] == jnp.arange(group_count)[None, :]).astype(jnp.float32)
    level_pick = (weight_index[:, None] == jnp.arange(level_count)[None, :]).astype(jnp.float32)
    group_weight = jnp.sum(level_pick * guidance_levels[None, :], axis=1)
    request_weight = jnp.sum(in_group * group_weight[None, :], axis=1)
    weight_rows = lax.dynamic_slice_in_dim(request_weight, stream_index * half_rows, half_rows, 0)
    logits = uncond + weight_rows[:, None] * (cond - uncond)
    return (logits, new_key[None], new_value[None])


TILE = 512
LANES = 128
MESH = pl.DeviceIdType.MESH
F32 = jnp.float32
BF16 = jnp.bfloat16
HIGH = lax.Precision.HIGHEST
PHASES = 8
QKV_SUM, QKV_ALL, ATT_SUM, ATT_STAT, OUT_SUM, MIX_ALL, EXP_SUM, FIN_ALL = range(PHASES)


def iota(shape, dim):
    return lax.broadcasted_iota(jnp.int32, shape, dim)


def step_kernel(
    n,
    nb,
    hidden,
    lengths,
    router,
    routes,
    group_ids,
    weight_index,
    levels,
    w_qkv,
    key_cache,
    value_cache,
    w_out,
    w_gate,
    w_up,
    w_down,
    w_vocab,
    logits_o,
    keys_o,
    values_o,
    qkv_v,
    key_v,
    value_v,
    out_v,
    gate_v,
    up_v,
    down_v,
    vocab_v,
    qkv_part,
    qkv_sum,
    qkv_all,
    att_part,
    att_sum,
    att_stat,
    out_part,
    out_sum,
    mix_all,
    exp_part,
    exp_sum,
    fin_all,
    final_own,
    final_all,
    load_sem,
    tile_sem,
    send_sem,
    recv_sem,
    fin_send,
    fin_recv,
):
    g = lax.axis_index("guide")
    b = lax.axis_index("blk")
    t = lax.axis_index("batch")
    half = nb // 2
    count, width = hidden.shape[1:]
    span = key_cache.shape[2]
    cols = width // n
    kv_width = key_cache.shape[3]
    group = HEADS // KV_HEADS
    tiles = gate_v.shape[0]
    vocab_tiles = vocab_v.shape[0]
    my_cols = pl.ds(pl.multiple_of(b * cols, LANES), cols)

    loads = [
        pltpu.make_async_copy(w_qkv, qkv_v, load_sem.at[0]),
        pltpu.make_async_copy(key_cache.at[0], key_v, load_sem.at[1]),
        pltpu.make_async_copy(value_cache.at[0], value_v, load_sem.at[2]),
        pltpu.make_async_copy(w_out, out_v, load_sem.at[3]),
    ]
    for load in loads:
        load.start()

    barrier = pltpu.get_barrier_semaphore()
    for k in range(1, n):
        pl.semaphore_signal(
            barrier, inc=1, device_id={"blk": lax.rem(b + k, n)}, device_id_type=MESH
        )
    for k in range(1, 2 * nb):
        other = lax.rem(g * nb + t + k, 2 * nb)
        pl.semaphore_signal(
            barrier,
            inc=1,
            device_id={"guide": other // nb, "batch": lax.rem(other, nb)},
            device_id_type=MESH,
        )

    def tile_cols(i):
        return pl.ds(pl.multiple_of(i * TILE, TILE), TILE)

    def gate_load(i):
        return pltpu.make_async_copy(w_gate.at[:, tile_cols(i)], gate_v.at[i], tile_sem.at[0, i])

    def up_load(i):
        return pltpu.make_async_copy(w_up.at[:, tile_cols(i)], up_v.at[i], tile_sem.at[1, i])

    def down_load(i):
        return pltpu.make_async_copy(w_down.at[tile_cols(i), :], down_v.at[i], tile_sem.at[2, i])

    def vocab_load(i):
        return pltpu.make_async_copy(w_vocab.at[:, tile_cols(i)], vocab_v.at[i], tile_sem.at[3, i])

    def send(phase, source, landing):
        for k in range(1, n):
            peer = lax.rem(b + k, n)
            pltpu.make_async_remote_copy(
                src_ref=source(peer),
                dst_ref=landing.at[b],
                send_sem=send_sem.at[phase, k - 1],
                recv_sem=recv_sem.at[phase, b],
                device_id={"blk": peer},
                device_id_type=MESH,
            ).start()

    def arrive(phase, landing):
        for k in range(1, n):
            peer = lax.rem(b + k, n)
            pltpu.make_async_remote_copy(
                src_ref=landing.at[peer],
                dst_ref=landing.at[peer],
                send_sem=send_sem.at[phase, k - 1],
                recv_sem=recv_sem.at[phase, peer],
                device_id={"blk": peer},
                device_id_type=MESH,
            ).wait_recv()

    def drain(phase, landing):
        for k in range(1, n):
            peer = lax.rem(b + k, n)
            pltpu.make_async_remote_copy(
                src_ref=landing.at[b],
                dst_ref=landing.at[b],
                send_sem=send_sem.at[phase, k - 1],
                recv_sem=recv_sem.at[phase, b],
                device_id={"blk": peer},
                device_id_type=MESH,
            ).wait_send()

    def summed(landing):
        total = landing[0].astype(F32)
        for j in range(1, n):
            total = total + landing[j].astype(F32)
        return total

    def joined(landing):
        return jnp.concatenate([landing[j] for j in range(n)], axis=1)

    def inverse_rms(values):
        return lax.rsqrt(jnp.mean(values * values, axis=-1, keepdims=True) + EPS)

    inverse = inverse_rms(hidden[0].astype(F32))
    normed = (hidden[0, :, my_cols].astype(F32) * inverse).astype(BF16)
    loads[0].wait()

    def start_expert(i, carry):
        gate_load(i).start()
        up_load(i).start()
        down_load(i).start()
        return carry

    def start_vocab(i, carry):
        vocab_load(i).start()
        return carry

    for j in range(n):
        starts = (
            (0, cols, j * cols),
            (cols, LANES, width + j * LANES),
            (cols + LANES, LANES, width + kv_width + j * LANES),
        )
        for at, size, begin in starts:
            qkv_part[j, :, at : at + size] = jnp.dot(
                normed, qkv_v[:, begin : begin + size], preferred_element_type=F32
            )
    qkv_sum[b] = qkv_part[b]
    pl.semaphore_wait(barrier, n - 1 + 2 * nb - 1)
    send(QKV_SUM, lambda peer: qkv_part.at[peer], qkv_sum)
    lax.fori_loop(0, tiles, start_expert, 0)
    lax.fori_loop(0, vocab_tiles, start_vocab, 0)

    kept = final_all.shape[0] // 2 * count
    row = iota((kept, 1), 0)

    def pick_weight(i, column):
        level = levels[weight_index[group_ids[g * kept + i]]]
        return jnp.where(row == i, level, column)

    weight = lax.fori_loop(0, kept, pick_weight, jnp.zeros((kept, 1), F32))

    low = iota((count, LANES), 1) < HEAD_DIM
    arrive(QKV_SUM, qkv_sum)
    total = summed(qkv_sum)
    va, vb, vc, vk, vv = (total[:, LANES * i : LANES * (i + 1)] for i in range(5))
    q0 = jnp.where(low, va, vb).astype(BF16)
    q1 = jnp.where(low, pltpu.roll(va, HEAD_DIM, 1), pltpu.roll(vc, HEAD_DIM, 1)).astype(BF16)
    q2 = jnp.where(low, vb, vc).astype(BF16)
    own_key = vk.astype(BF16)
    own_value = vv.astype(BF16)
    qkv_all[b] = jnp.concatenate([q0, q1, q2, own_key, own_value], axis=1)
    send(QKV_ALL, lambda peer: qkv_all.at[b], qkv_all)

    scale = HEAD_DIM ** (-0.5)
    same_head = (
        iota((LANES, LANES), 0) // HEAD_DIM == iota((LANES, LANES), 1) // HEAD_DIM
    ).astype(F32)
    own_score = jnp.concatenate(
        [
            jnp.dot(
                q.astype(F32) * own_key.astype(F32),
                same_head,
                precision=HIGH,
                preferred_element_type=F32,
            )
            for q in (q0, q1, q2)
        ],
        axis=1,
    ) * scale
    own_value3 = jnp.concatenate([own_value.astype(F32)] * group, axis=1)
    heads = group * KV_HEADS
    rows = count * heads
    places = count * span
    place = iota((1, places), 1)
    limit = jnp.zeros((1, places), jnp.int32)
    for r in range(count):
        limit = jnp.where(place // span == r, lengths[0, r], limit)
    in_cache = b * span + lax.rem(place, span) < limit
    valid = jnp.logical_and(iota((rows, 1), 0) // heads == place // span, in_cache)
    head_lanes = (
        iota((KV_HEADS, kv_width), 1) // HEAD_DIM == iota((KV_HEADS, kv_width), 0)
    ).astype(F32)[None]
    loads[1].wait()
    loads[2].wait()

    arrive(QKV_ALL, qkv_all)
    for j in range(n):
        spot = slice(LANES * j, LANES * (j + 1))
        keys_o[0, :, spot] = qkv_all[j, :, cols : cols + LANES]
        values_o[0, :, spot] = qkv_all[j, :, cols + LANES : cols + 2 * LANES]
    spread = []
    for i in range(group):
        query = jnp.concatenate(
            [qkv_all[j, :, LANES * i : LANES * (i + 1)] for j in range(n)], axis=1
        )
        spread.append(query.astype(F32)[:, None, :] * head_lanes)
    spread = jnp.concatenate(spread, axis=1).reshape(rows, kv_width).astype(BF16)
    scores = (
        lax.dot_general(
            spread,
            key_v[...].reshape(places, kv_width),
            (((1,), (1,)), ((), ())),
            preferred_element_type=F32,
        )
        * scale
    )
    top = jnp.max(jnp.where(valid, scores, -1e30), axis=1, keepdims=True)
    probs = jnp.exp(jnp.where(valid, scores - top, -1e30))
    mass = jnp.sum(probs, axis=1, keepdims=True)
    acc = jnp.dot(
        probs.astype(BF16), value_v[...].reshape(places, kv_width), preferred_element_type=F32
    ).reshape(count, heads, kv_width)
    for i in range(group):
        mine = jnp.sum(acc[:, KV_HEADS * i : KV_HEADS * (i + 1), :] * head_lanes, axis=1)
        for j in range(n):
            att_part[j, :, LANES * i : LANES * (i + 1)] = mine[
                :, LANES * j : LANES * (j + 1)
            ].astype(BF16)
    lane = iota((heads, LANES), 1)
    slot = iota((heads, LANES), 0)
    packed = jnp.where(lane[None] == slot[None], top.reshape(count, heads, 1), 0.0) + jnp.where(
        lane[None] == slot[None] + HEAD_DIM, mass.reshape(count, heads, 1), 0.0
    )
    att_stat[b] = jnp.sum(packed, axis=1)
    att_sum[b] = att_part[b]
    send(ATT_STAT, lambda peer: att_stat.at[b], att_stat)
    send(ATT_SUM, lambda peer: att_part.at[peer], att_sum)

    from_lane = iota((LANES, cols), 0)
    to_lane = iota((LANES, cols), 1)
    head_of = (
        to_lane // LANES * KV_HEADS
        + b * (KV_HEADS // n)
        + lax.rem(to_lane, LANES) // HEAD_DIM
    )
    pick_top = (from_lane == head_of).astype(F32)
    pick_mass = (from_lane == head_of + HEAD_DIM).astype(F32)
    loads[3].wait()
    arrive(ATT_STAT, att_stat)
    stats = att_stat[...].reshape(n * count, LANES)
    tops = jnp.dot(stats, pick_top, precision=HIGH, preferred_element_type=F32)
    masses = jnp.dot(stats, pick_mass, precision=HIGH, preferred_element_type=F32)
    best = own_score
    for j in range(n):
        best = jnp.maximum(best, tops[count * j : count * (j + 1)])
    own_prob = jnp.exp(own_score - best)
    denominator = own_prob
    numerator = own_prob.astype(BF16).astype(F32) * own_value3
    arrive(ATT_SUM, att_sum)
    for j in range(n):
        share = jnp.exp(tops[count * j : count * (j + 1)] - best)
        denominator = denominator + share * masses[count * j : count * (j + 1)]
        numerator = numerator + share * att_sum[j].astype(F32)
    a0, a1, a2 = (
        (numerator / denominator)[:, LANES * i : LANES * (i + 1)] for i in range(group)
    )
    turned = pltpu.roll(a1, HEAD_DIM, 1)
    attn = jnp.concatenate(
        [jnp.where(low, a0, turned), jnp.where(low, a2, a0), jnp.where(low, turned, a2)], axis=1
    ).astype(BF16)
    for j in range(n):
        out_part[j] = jnp.dot(
            attn, out_v[:, cols * j : cols * (j + 1)], preferred_element_type=F32
        ).astype(BF16)
    out_sum[b] = out_part[b]
    send(OUT_SUM, lambda peer: out_part.at[peer], out_sum)
    arrive(OUT_SUM, out_sum)
    mixed = hidden[0, :, my_cols].astype(F32) + summed(out_sum)
    mix_all[b] = mixed.astype(BF16)
    send(MIX_ALL, lambda peer: mix_all.at[b], mix_all)
    arrive(MIX_ALL, mix_all)

    expert_in = joined(mix_all)
    inverse = inverse_rms(expert_in.astype(F32))
    choice = jnp.dot(expert_in, router[...], preferred_element_type=F32) * inverse
    expert = iota((count, EXPERTS), 1)
    is_first = (expert == routes[0, :, 0:1]).astype(F32)
    is_second = (expert == routes[0, :, 1:2]).astype(F32)
    gap = jnp.sum((is_first - is_second) * choice, axis=1, keepdims=True)
    first = 1.0 / (1.0 + jnp.exp(-gap))
    per_expert = is_first * first + is_second * (1.0 - first)

    def expert_tile(i, out):
        gate_load(i).wait()
        gate = jnp.dot(expert_in, gate_v[i], preferred_element_type=F32) * inverse
        up_load(i).wait()
        upper = jnp.dot(expert_in, up_v[i], preferred_element_type=F32) * inverse
        owner = (b * tiles + i) * TILE // EXPERT_UNITS
        share = jnp.sum(jnp.where(expert == owner, per_expert, 0.0), axis=1, keepdims=True)
        act = (gate / (1.0 + jnp.exp(-gate)) * upper * share).astype(BF16)
        down_load(i).wait()
        return out + jnp.dot(act, down_v[i], preferred_element_type=F32)

    expert_out = lax.fori_loop(0, tiles, expert_tile, jnp.zeros((count, width), F32))
    for j in range(n):
        exp_part[j] = expert_out[:, cols * j : cols * (j + 1)].astype(BF16)
    exp_sum[b] = exp_part[b]
    send(EXP_SUM, lambda peer: exp_part.at[peer], exp_sum)
    arrive(EXP_SUM, exp_sum)
    fin_all[b] = (mixed + summed(exp_sum)).astype(BF16)
    send(FIN_ALL, lambda peer: fin_all.at[b], fin_all)
    arrive(FIN_ALL, fin_all)
    final_own[...] = joined(fin_all)

    def final_copy(to_batch, landing_slot, send_slot):
        return pltpu.make_async_remote_copy(
            src_ref=final_own,
            dst_ref=final_all.at[landing_slot],
            send_sem=fin_send.at[send_slot],
            recv_sem=fin_recv.at[landing_slot],
            device_id={"guide": t // half, "batch": to_batch},
            device_id_type=MESH,
        )

    my_slot = g * half + lax.rem(t, half)
    stays = g == t // half
    for k in range(1, nb):
        final_copy(lax.rem(t + k, nb), my_slot, k).start()

    @pl.when(stays)
    def _():
        final_all[my_slot] = final_own[...]

    @pl.when(jnp.logical_not(stays))
    def _():
        final_copy(t, my_slot, 0).start()

    for s in range(2):
        for j in range(half):
            from_me = jnp.logical_and(g == s, t == g * half + j)

            @pl.when(jnp.logical_not(from_me))
            def _():
                final_copy(t, s * half + j, 0).wait_recv()

    finals = final_all[...].reshape(2 * half * count, width)
    inverse = inverse_rms(finals.astype(F32))

    def vocab_tile(i, carry):
        vocab_load(i).wait()
        streams = jnp.dot(finals, vocab_v[i], preferred_element_type=F32) * inverse
        cond, uncond = streams[:kept], streams[kept:]
        logits_o[:, tile_cols(i)] = uncond + weight * (cond - uncond)
        return carry

    lax.fori_loop(0, vocab_tiles, vocab_tile, 0)

    for phase, landing in (
        (QKV_SUM, qkv_sum),
        (QKV_ALL, qkv_all),
        (ATT_SUM, att_sum),
        (ATT_STAT, att_stat),
        (OUT_SUM, out_sum),
        (MIX_ALL, mix_all),
        (EXP_SUM, exp_sum),
        (FIN_ALL, fin_all),
    ):
        drain(phase, landing)
    for k in range(1, nb):
        final_copy(lax.rem(t + k, nb), my_slot, k).wait_send()

    @pl.when(jnp.logical_not(stays))
    def _():
        final_copy(t, my_slot, 0).wait_send()


def local_kernel(
    n,
    nb,
    hidden,
    w_qkv,
    key_cache,
    value_cache,
    lengths,
    w_out,
    router,
    routes,
    w_gate,
    w_up,
    w_down,
    w_vocab,
    group_ids,
    weight_index,
    guidance_levels,
):
    count, width = hidden.shape[1:]
    span, kv_width = key_cache.shape[2:]
    cols = width // n
    units = w_gate.shape[1]
    vocab = w_vocab.shape[1]
    half = nb // 2
    kept = half * count
    vmem = pl.BlockSpec(memory_space=pltpu.VMEM)
    smem = pl.BlockSpec(memory_space=pltpu.SMEM)
    anywhere = pl.BlockSpec(memory_space=pl.ANY)
    packed = cols + 2 * LANES
    chunk = pltpu.VMEM((n, count, cols), BF16)
    tiles, vocab_tiles = units // TILE, vocab // TILE
    weights = 2 * (3 * width * units + width * vocab + w_qkv.size + w_out.size)
    return pl.pallas_call(
        functools.partial(step_kernel, n, nb),
        out_shape=(
            jax.ShapeDtypeStruct((kept, vocab), F32),
            jax.ShapeDtypeStruct((1, count, kv_width), BF16),
            jax.ShapeDtypeStruct((1, count, kv_width), BF16),
        ),
        in_specs=[vmem, smem, vmem, vmem, smem, smem, smem] + [anywhere] * 8,
        out_specs=(vmem, vmem, vmem),
        scratch_shapes=[
            pltpu.VMEM(w_qkv.shape, BF16),
            pltpu.VMEM(key_cache.shape[1:], BF16),
            pltpu.VMEM(value_cache.shape[1:], BF16),
            pltpu.VMEM(w_out.shape, BF16),
            pltpu.VMEM((tiles, width, TILE), BF16),
            pltpu.VMEM((tiles, width, TILE), BF16),
            pltpu.VMEM((tiles, TILE, width), BF16),
            pltpu.VMEM((vocab_tiles, width, TILE), BF16),
            pltpu.VMEM((n, count, packed), F32),
            pltpu.VMEM((n, count, packed), F32),
            pltpu.VMEM((n, count, packed), BF16),
            chunk,
            chunk,
            pltpu.VMEM((n, count, LANES), F32),
            chunk,
            chunk,
            chunk,
            chunk,
            chunk,
            chunk,
            pltpu.VMEM((count, width), BF16),
            pltpu.VMEM((2 * half, count, width), BF16),
            pltpu.SemaphoreType.DMA((4,)),
            pltpu.SemaphoreType.DMA((4, max(tiles, vocab_tiles))),
            pltpu.SemaphoreType.DMA((PHASES, n)),
            pltpu.SemaphoreType.DMA((PHASES, n)),
            pltpu.SemaphoreType.DMA((nb,)),
            pltpu.SemaphoreType.DMA((2 * half,)),
        ],
        compiler_params=pltpu.CompilerParams(
            collective_id=0, has_side_effects=True, vmem_limit_bytes=60 * 2**20
        ),
        cost_estimate=pl.CostEstimate(
            flops=weights * count, bytes_accessed=weights, transcendentals=count * units
        ),
    )(
        hidden,
        lengths,
        router,
        routes,
        group_ids,
        weight_index,
        guidance_levels,
        w_qkv,
        key_cache,
        value_cache,
        w_out,
        w_gate,
        w_up,
        w_down,
        w_vocab,
    )


def fits_kernel(mesh):
    return KV_HEADS * HEAD_DIM == mesh.shape["blk"] * LANES and mesh.shape["batch"] % 2 == 0


def solution(mesh):
    if fits_kernel(mesh):
        body = functools.partial(local_kernel, mesh.shape["blk"], mesh.shape["batch"])
    else:
        body = local
    placed = (
        P("guide", "batch", None),
        P("blk", None),
        P("guide", "batch", "blk", None),
        P("guide", "batch", "blk", None),
        P("guide", "batch"),
        P("blk", None),
        P(),
        P("guide", "batch", None),
        P(None, "blk"),
        P(None, "blk"),
        P("blk", None),
        P(None, ("blk", "batch")),
        P(),
        P(),
        P(),
    )
    return jax.shard_map(
        body,
        mesh=mesh,
        in_specs=placed,
        out_specs=(
            P("guide", ("blk", "batch")),
            P("guide", "batch", None),
            P("guide", "batch", None),
        ),
        check_vma=False,
    )
```

```python
import functools

import jax
import jax.numpy as jnp
from jax import lax
from jax.experimental import pallas as pl
from jax.experimental.pallas import tpu as pltpu
from jax.sharding import PartitionSpec as P

HEADS = 24
KV_HEADS = 8
HEAD_DIM = 64
EXPERTS = 16
EXPERT_UNITS = 1024


EPS = 1e-05


def from_partner(value, axis, bit):
    mask = 2**bit
    pairs = [(source, source ^ mask) for source in range(lax.axis_size(axis))]
    return lax.ppermute(value, axis, pairs)


def rms(values):
    return values * lax.rsqrt(jnp.mean(values * values, axis=-1, keepdims=True) + EPS)


def local(
    hidden,
    w_qkv,
    key_cache,
    value_cache,
    lengths,
    w_out,
    router,
    routes,
    w_gate,
    w_up,
    w_down,
    w_vocab,
    group_ids,
    weight_index,
    guidance_levels,
):
    width_q = HEADS * HEAD_DIM
    width_k = KV_HEADS * HEAD_DIM
    group = HEADS // KV_HEADS
    position_block = lax.axis_index("blk")
    count = hidden.shape[1]
    x = hidden[0].astype(jnp.float32)
    normed = rms(x).astype(jnp.bfloat16)
    feat_rows = w_qkv.shape[0]
    normed_part = lax.dynamic_slice_in_dim(normed, position_block * feat_rows, feat_rows, 1)
    partial_qkv = jnp.dot(normed_part, w_qkv, preferred_element_type=jnp.float32)
    qkv = lax.psum(partial_qkv, "blk").astype(jnp.bfloat16)
    query = qkv[:, :width_q]
    new_key = qkv[:, width_q : width_q + width_k]
    new_value = qkv[:, width_q + width_k :]
    span = key_cache.shape[2]
    query_heads = query.reshape(count, KV_HEADS, group, HEAD_DIM)
    keys_here = key_cache[0].reshape(count, span, KV_HEADS, HEAD_DIM)
    values_here = value_cache[0].reshape(count, span, KV_HEADS, HEAD_DIM)
    scale = HEAD_DIM ** (-0.5)
    scores = (
        jnp.einsum("rkgd,rckd->rkgc", query_heads, keys_here, preferred_element_type=jnp.float32)
        * scale
    )
    own = (
        jnp.einsum(
            "rkgd,rkd->rkg",
            query_heads,
            new_key.reshape(count, KV_HEADS, HEAD_DIM),
            preferred_element_type=jnp.float32,
        )
        * scale
    )
    positions = position_block * span + jnp.arange(span)
    valid = (positions[None, :] < lengths[0][:, None])[:, None, None, :]
    local_top = jnp.max(jnp.where(valid, scores, -1e30), axis=-1)
    top = lax.pmax(jnp.maximum(local_top, own), "blk")
    probs = jnp.exp(jnp.where(valid, scores - top[..., None], -1e30))
    partial_total = jnp.sum(probs, axis=-1)
    acc = jnp.einsum(
        "rkgc,rckd->rkgd",
        probs.astype(jnp.bfloat16),
        values_here,
        preferred_element_type=jnp.float32,
    ).reshape(count, width_q)
    own_prob = jnp.exp(own - top)
    own_rounded = lax.optimization_barrier(own_prob.astype(jnp.bfloat16)).astype(jnp.float32)
    own_term = (
        own_rounded[..., None] * new_value.astype(jnp.float32).reshape(count, KV_HEADS, 1, HEAD_DIM)
    ).reshape(count, width_q)
    out_rows = w_out.shape[0]
    acc_sum, total_sum = lax.psum((acc, partial_total), "blk")
    totals = jnp.repeat((total_sum + own_prob).reshape(count, HEADS), HEAD_DIM, axis=1)
    attn = ((acc_sum + own_term) / totals).astype(jnp.bfloat16)
    attn_cols = lax.dynamic_slice_in_dim(attn, position_block * out_rows, out_rows, 1)
    mixed = x + lax.psum(jnp.dot(attn_cols, w_out, preferred_element_type=jnp.float32), "blk")
    expert_in = rms(mixed).astype(jnp.bfloat16)
    choice_logits = jnp.dot(expert_in, router, preferred_element_type=jnp.float32)
    picks = (routes[0][:, :, None] == jnp.arange(EXPERTS)[None, None, :]).astype(jnp.float32)
    chosen = jnp.sum(picks * choice_logits[:, None, :], axis=-1)
    first = jax.nn.sigmoid(chosen[:, 0] - chosen[:, 1])
    shares = jnp.stack([first, 1.0 - first], axis=1)
    per_expert = jnp.sum(picks * shares[:, :, None], axis=1)
    local_units = w_gate.shape[1]
    owner = (position_block * local_units + jnp.arange(local_units)) // EXPERT_UNITS
    member = (owner[None, :] == jnp.arange(EXPERTS)[:, None]).astype(jnp.float32)
    unit_weight = jnp.sum(per_expert[:, :, None] * member[None, :, :], axis=1)
    gate = jnp.dot(expert_in, w_gate, preferred_element_type=jnp.float32)
    upper = jnp.dot(expert_in, w_up, preferred_element_type=jnp.float32)
    act = (jax.nn.silu(gate) * upper * unit_weight).astype(jnp.bfloat16)
    expert_out = lax.psum(jnp.dot(act, w_down, preferred_element_type=jnp.float32), "blk")
    final_in = rms(mixed + expert_out).astype(jnp.bfloat16)
    stream_logits = jnp.dot(
        lax.all_gather(final_in, "batch", axis=0, tiled=True),
        w_vocab,
        preferred_element_type=jnp.float32,
    ).astype(jnp.bfloat16)
    stream_index = lax.axis_index("guide")
    half_rows = stream_logits.shape[0] // 2
    kept_rows = lax.dynamic_slice_in_dim(stream_logits, stream_index * half_rows, half_rows, 0)
    sent_rows = lax.dynamic_slice_in_dim(
        stream_logits, (1 - stream_index) * half_rows, half_rows, 0
    )
    partner = from_partner(sent_rows, "guide", 0)
    is_first = stream_index == 0
    cond = jnp.where(is_first, kept_rows, partner).astype(jnp.float32)
    uncond = jnp.where(is_first, partner, kept_rows).astype(jnp.float32)
    group_count = weight_index.shape[0]
    level_count = guidance_levels.shape[0]
    in_group = (group_ids[:, None] == jnp.arange(group_count)[None, :]).astype(jnp.float32)
    level_pick = (weight_index[:, None] == jnp.arange(level_count)[None, :]).astype(jnp.float32)
    group_weight = jnp.sum(level_pick * guidance_levels[None, :], axis=1)
    request_weight = jnp.sum(in_group * group_weight[None, :], axis=1)
    weight_rows = lax.dynamic_slice_in_dim(request_weight, stream_index * half_rows, half_rows, 0)
    logits = uncond + weight_rows[:, None] * (cond - uncond)
    return (logits, new_key[None], new_value[None])


TILE = 512
LANES = 128
MESH = pl.DeviceIdType.MESH
F32 = jnp.float32
BF16 = jnp.bfloat16
HIGH = lax.Precision.HIGHEST
PHASES = 8
QKV_SUM, QKV_ALL, ATT_SUM, ATT_STAT, OUT_SUM, MIX_ALL, EXP_SUM, FIN_ALL = range(PHASES)


def iota(shape, dim):
    return lax.broadcasted_iota(jnp.int32, shape, dim)


def step_kernel(
    n,
    nb,
    hidden,
    lengths,
    router,
    routes,
    group_ids,
    weight_index,
    levels,
    w_qkv,
    key_cache,
    value_cache,
    w_out,
    w_gate,
    w_up,
    w_down,
    w_vocab,
    logits_o,
    keys_o,
    values_o,
    qkv_v,
    key_v,
    value_v,
    out_v,
    gate_v,
    up_v,
    down_v,
    vocab_v,
    qkv_part,
    qkv_sum,
    qkv_all,
    att_part,
    att_sum,
    att_stat,
    out_part,
    out_sum,
    mix_all,
    exp_part,
    exp_sum,
    fin_all,
    final_own,
    final_all,
    load_sem,
    tile_sem,
    send_sem,
    recv_sem,
    fin_send,
    fin_recv,
):
    g = lax.axis_index("guide")
    b = lax.axis_index("blk")
    t = lax.axis_index("batch")
    half = nb // 2
    count, width = hidden.shape[1:]
    span = key_cache.shape[2]
    cols = width // n
    kv_width = key_cache.shape[3]
    group = HEADS // KV_HEADS
    tiles = gate_v.shape[0]
    vocab_tiles = vocab_v.shape[0]
    my_cols = pl.ds(pl.multiple_of(b * cols, LANES), cols)

    loads = [
        pltpu.make_async_copy(w_qkv, qkv_v, load_sem.at[0]),
        pltpu.make_async_copy(key_cache.at[0], key_v, load_sem.at[1]),
        pltpu.make_async_copy(value_cache.at[0], value_v, load_sem.at[2]),
        pltpu.make_async_copy(w_out, out_v, load_sem.at[3]),
    ]
    for load in loads:
        load.start()

    barrier = pltpu.get_barrier_semaphore()
    for k in range(1, n):
        pl.semaphore_signal(
            barrier, inc=1, device_id={"blk": lax.rem(b + k, n)}, device_id_type=MESH
        )
    for k in range(1, 2 * nb):
        other = lax.rem(g * nb + t + k, 2 * nb)
        pl.semaphore_signal(
            barrier,
            inc=1,
            device_id={"guide": other // nb, "batch": lax.rem(other, nb)},
            device_id_type=MESH,
        )

    def tile_cols(i):
        return pl.ds(pl.multiple_of(i * TILE, TILE), TILE)

    def gate_load(i):
        return pltpu.make_async_copy(w_gate.at[:, tile_cols(i)], gate_v.at[i], tile_sem.at[0, i])

    def up_load(i):
        return pltpu.make_async_copy(w_up.at[:, tile_cols(i)], up_v.at[i], tile_sem.at[1, i])

    def down_load(i):
        return pltpu.make_async_copy(w_down.at[tile_cols(i), :], down_v.at[i], tile_sem.at[2, i])

    def vocab_load(i):
        return pltpu.make_async_copy(w_vocab.at[:, tile_cols(i)], vocab_v.at[i], tile_sem.at[3, i])

    def send(phase, source, landing):
        for k in range(1, n):
            peer = lax.rem(b + k, n)
            pltpu.make_async_remote_copy(
                src_ref=source(peer),
                dst_ref=landing.at[b],
                send_sem=send_sem.at[phase, k - 1],
                recv_sem=recv_sem.at[phase, b],
                device_id={"blk": peer},
                device_id_type=MESH,
            ).start()

    def arrive(phase, landing):
        for k in range(1, n):
            peer = lax.rem(b + k, n)
            pltpu.make_async_remote_copy(
                src_ref=landing.at[peer],
                dst_ref=landing.at[peer],
                send_sem=send_sem.at[phase, k - 1],
                recv_sem=recv_sem.at[phase, peer],
                device_id={"blk": peer},
                device_id_type=MESH,
            ).wait_recv()

    def drain(phase, landing):
        for k in range(1, n):
            peer = lax.rem(b + k, n)
            pltpu.make_async_remote_copy(
                src_ref=landing.at[b],
                dst_ref=landing.at[b],
                send_sem=send_sem.at[phase, k - 1],
                recv_sem=recv_sem.at[phase, b],
                device_id={"blk": peer},
                device_id_type=MESH,
            ).wait_send()

    def summed(landing):
        total = landing[0].astype(F32)
        for j in range(1, n):
            total = total + landing[j].astype(F32)
        return total

    def joined(landing):
        return jnp.concatenate([landing[j] for j in range(n)], axis=1)

    def inverse_rms(values):
        return lax.rsqrt(jnp.mean(values * values, axis=-1, keepdims=True) + EPS)

    inverse = inverse_rms(hidden[0].astype(F32))
    normed = (hidden[0, :, my_cols].astype(F32) * inverse).astype(BF16)
    loads[0].wait()

    def start_expert(i, carry):
        gate_load(i).start()
        up_load(i).start()
        down_load(i).start()
        return carry

    def start_vocab(i, carry):
        vocab_load(i).start()
        return carry

    for j in range(n):
        starts = (
            (0, cols, j * cols),
            (cols, LANES, width + j * LANES),
            (cols + LANES, LANES, width + kv_width + j * LANES),
        )
        for at, size, begin in starts:
            qkv_part[j, :, at : at + size] = jnp.dot(
                normed, qkv_v[:, begin : begin + size], preferred_element_type=F32
            )
    qkv_sum[b] = qkv_part[b]
    pl.semaphore_wait(barrier, n - 1 + 2 * nb - 1)
    send(QKV_SUM, lambda peer: qkv_part.at[peer], qkv_sum)
    lax.fori_loop(0, tiles, start_expert, 0)
    lax.fori_loop(0, vocab_tiles, start_vocab, 0)

    kept = final_all.shape[0] // 2 * count
    row = iota((kept, 1), 0)

    def pick_weight(i, column):
        level = levels[weight_index[group_ids[g * kept + i]]]
        return jnp.where(row == i, level, column)

    weight = lax.fori_loop(0, kept, pick_weight, jnp.zeros((kept, 1), F32))

    request = iota((count, 1), 0)
    chosen_first = jnp.zeros((count, 1), jnp.int32)
    chosen_second = jnp.zeros((count, 1), jnp.int32)
    for r in range(count):
        chosen_first = jnp.where(request == r, routes[0, 0, r], chosen_first)
        chosen_second = jnp.where(request == r, routes[0, 1, r], chosen_second)

    low = iota((count, LANES), 1) < HEAD_DIM
    arrive(QKV_SUM, qkv_sum)
    total = summed(qkv_sum)
    va, vb, vc, vk, vv = (total[:, LANES * i : LANES * (i + 1)] for i in range(5))
    q0 = jnp.where(low, va, vb).astype(BF16)
    q1 = jnp.where(low, pltpu.roll(va, HEAD_DIM, 1), pltpu.roll(vc, HEAD_DIM, 1)).astype(BF16)
    q2 = jnp.where(low, vb, vc).astype(BF16)
    own_key = vk.astype(BF16)
    own_value = vv.astype(BF16)
    qkv_all[b] = jnp.concatenate([q0, q1, q2, own_key, own_value], axis=1)
    send(QKV_ALL, lambda peer: qkv_all.at[b], qkv_all)

    scale = HEAD_DIM ** (-0.5)
    same_head = (
        iota((LANES, LANES), 0) // HEAD_DIM == iota((LANES, LANES), 1) // HEAD_DIM
    ).astype(F32)
    own_score = jnp.concatenate(
        [
            jnp.dot(
                q.astype(F32) * own_key.astype(F32),
                same_head,
                precision=HIGH,
                preferred_element_type=F32,
            )
            for q in (q0, q1, q2)
        ],
        axis=1,
    ) * scale
    own_value3 = jnp.concatenate([own_value.astype(F32)] * group, axis=1)
    heads = group * KV_HEADS
    rows = count * heads
    places = count * span
    place = iota((1, places), 1)
    limit = jnp.zeros((1, places), jnp.int32)
    for r in range(count):
        limit = jnp.where(place // span == r, lengths[0, r], limit)
    in_cache = b * span + lax.rem(place, span) < limit
    valid = jnp.logical_and(iota((rows, 1), 0) // heads == place // span, in_cache)
    head_lanes = (
        iota((KV_HEADS, kv_width), 1) // HEAD_DIM == iota((KV_HEADS, kv_width), 0)
    ).astype(F32)[None]
    loads[1].wait()
    loads[2].wait()

    arrive(QKV_ALL, qkv_all)
    for j in range(n):
        spot = slice(LANES * j, LANES * (j + 1))
        keys_o[0, :, spot] = qkv_all[j, :, cols : cols + LANES]
        values_o[0, :, spot] = qkv_all[j, :, cols + LANES : cols + 2 * LANES]
    spread = []
    for i in range(group):
        query = jnp.concatenate(
            [qkv_all[j, :, LANES * i : LANES * (i + 1)] for j in range(n)], axis=1
        )
        spread.append(query.astype(F32)[:, None, :] * head_lanes)
    spread = jnp.concatenate(spread, axis=1).reshape(rows, kv_width).astype(BF16)
    scores = (
        lax.dot_general(
            spread,
            key_v[...].reshape(places, kv_width),
            (((1,), (1,)), ((), ())),
            preferred_element_type=F32,
        )
        * scale
    )
    top = jnp.max(jnp.where(valid, scores, -1e30), axis=1, keepdims=True)
    probs = jnp.exp(jnp.where(valid, scores - top, -1e30))
    mass = jnp.sum(probs, axis=1, keepdims=True)
    acc = jnp.dot(
        probs.astype(BF16), value_v[...].reshape(places, kv_width), preferred_element_type=F32
    ).reshape(count, heads, kv_width)
    for i in range(group):
        mine = jnp.sum(acc[:, KV_HEADS * i : KV_HEADS * (i + 1), :] * head_lanes, axis=1)
        for j in range(n):
            att_part[j, :, LANES * i : LANES * (i + 1)] = mine[
                :, LANES * j : LANES * (j + 1)
            ].astype(BF16)
    lane = iota((heads, LANES), 1)
    slot = iota((heads, LANES), 0)
    packed = jnp.where(lane[None] == slot[None], top.reshape(count, heads, 1), 0.0) + jnp.where(
        lane[None] == slot[None] + HEAD_DIM, mass.reshape(count, heads, 1), 0.0
    )
    att_stat[b] = jnp.sum(packed, axis=1)
    att_sum[b] = att_part[b]
    send(ATT_STAT, lambda peer: att_stat.at[b], att_stat)
    send(ATT_SUM, lambda peer: att_part.at[peer], att_sum)

    from_lane = iota((LANES, cols), 0)
    to_lane = iota((LANES, cols), 1)
    head_of = (
        to_lane // LANES * KV_HEADS
        + b * (KV_HEADS // n)
        + lax.rem(to_lane, LANES) // HEAD_DIM
    )
    pick_top = (from_lane == head_of).astype(F32)
    pick_mass = (from_lane == head_of + HEAD_DIM).astype(F32)
    loads[3].wait()
    arrive(ATT_STAT, att_stat)
    stats = att_stat[...].reshape(n * count, LANES)
    tops = jnp.dot(stats, pick_top, precision=HIGH, preferred_element_type=F32)
    masses = jnp.dot(stats, pick_mass, precision=HIGH, preferred_element_type=F32)
    best = own_score
    for j in range(n):
        best = jnp.maximum(best, tops[count * j : count * (j + 1)])
    own_prob = jnp.exp(own_score - best)
    denominator = own_prob
    numerator = own_prob.astype(BF16).astype(F32) * own_value3
    arrive(ATT_SUM, att_sum)
    for j in range(n):
        share = jnp.exp(tops[count * j : count * (j + 1)] - best)
        denominator = denominator + share * masses[count * j : count * (j + 1)]
        numerator = numerator + share * att_sum[j].astype(F32)
    a0, a1, a2 = (
        (numerator / denominator)[:, LANES * i : LANES * (i + 1)] for i in range(group)
    )
    turned = pltpu.roll(a1, HEAD_DIM, 1)
    attn = jnp.concatenate(
        [jnp.where(low, a0, turned), jnp.where(low, a2, a0), jnp.where(low, turned, a2)], axis=1
    ).astype(BF16)
    for j in range(n):
        out_part[j] = jnp.dot(
            attn, out_v[:, cols * j : cols * (j + 1)], preferred_element_type=F32
        ).astype(BF16)
    out_sum[b] = out_part[b]
    send(OUT_SUM, lambda peer: out_part.at[peer], out_sum)
    arrive(OUT_SUM, out_sum)
    mixed = hidden[0, :, my_cols].astype(F32) + summed(out_sum)
    mix_all[b] = mixed.astype(BF16)
    send(MIX_ALL, lambda peer: mix_all.at[b], mix_all)
    arrive(MIX_ALL, mix_all)

    expert_in = joined(mix_all)
    inverse = inverse_rms(expert_in.astype(F32))
    choice = (
        lax.dot_general(
            expert_in, router[...], (((1,), (1,)), ((), ())), preferred_element_type=F32
        )
        * inverse
    )
    expert = iota((count, EXPERTS), 1)
    is_first = (expert == chosen_first).astype(F32)
    is_second = (expert == chosen_second).astype(F32)
    gap = jnp.sum((is_first - is_second) * choice, axis=1, keepdims=True)
    first = 1.0 / (1.0 + jnp.exp(-gap))
    per_expert = is_first * first + is_second * (1.0 - first)

    def expert_tile(i, out):
        gate_load(i).wait()
        gate = jnp.dot(expert_in, gate_v[i], preferred_element_type=F32) * inverse
        up_load(i).wait()
        upper = jnp.dot(expert_in, up_v[i], preferred_element_type=F32) * inverse
        owner = (b * tiles + i) * TILE // EXPERT_UNITS
        share = jnp.sum(jnp.where(expert == owner, per_expert, 0.0), axis=1, keepdims=True)
        act = (gate / (1.0 + jnp.exp(-gate)) * upper * share).astype(BF16)
        down_load(i).wait()
        return out + jnp.dot(act, down_v[i], preferred_element_type=F32)

    expert_out = lax.fori_loop(0, tiles, expert_tile, jnp.zeros((count, width), F32))
    for j in range(n):
        exp_part[j] = expert_out[:, cols * j : cols * (j + 1)].astype(BF16)
    exp_sum[b] = exp_part[b]
    send(EXP_SUM, lambda peer: exp_part.at[peer], exp_sum)
    arrive(EXP_SUM, exp_sum)
    fin_all[b] = (mixed + summed(exp_sum)).astype(BF16)
    send(FIN_ALL, lambda peer: fin_all.at[b], fin_all)
    arrive(FIN_ALL, fin_all)
    final_own[...] = joined(fin_all)

    def final_copy(to_batch, landing_slot, send_slot):
        return pltpu.make_async_remote_copy(
            src_ref=final_own,
            dst_ref=final_all.at[landing_slot],
            send_sem=fin_send.at[send_slot],
            recv_sem=fin_recv.at[landing_slot],
            device_id={"guide": t // half, "batch": to_batch},
            device_id_type=MESH,
        )

    my_slot = g * half + lax.rem(t, half)
    stays = g == t // half
    for k in range(1, nb):
        final_copy(lax.rem(t + k, nb), my_slot, k).start()

    @pl.when(stays)
    def _():
        final_all[my_slot] = final_own[...]

    @pl.when(jnp.logical_not(stays))
    def _():
        final_copy(t, my_slot, 0).start()

    for s in range(2):
        for j in range(half):
            from_me = jnp.logical_and(g == s, t == g * half + j)

            @pl.when(jnp.logical_not(from_me))
            def _():
                final_copy(t, s * half + j, 0).wait_recv()

    finals = final_all[...].reshape(2 * half * count, width)
    inverse = inverse_rms(finals.astype(F32))

    def vocab_tile(i, carry):
        vocab_load(i).wait()
        streams = jnp.dot(finals, vocab_v[i], preferred_element_type=F32) * inverse
        cond, uncond = streams[:kept], streams[kept:]
        logits_o[:, tile_cols(i)] = uncond + weight * (cond - uncond)
        return carry

    lax.fori_loop(0, vocab_tiles, vocab_tile, 0)

    for phase, landing in (
        (QKV_SUM, qkv_sum),
        (QKV_ALL, qkv_all),
        (ATT_SUM, att_sum),
        (ATT_STAT, att_stat),
        (OUT_SUM, out_sum),
        (MIX_ALL, mix_all),
        (EXP_SUM, exp_sum),
        (FIN_ALL, fin_all),
    ):
        drain(phase, landing)
    for k in range(1, nb):
        final_copy(lax.rem(t + k, nb), my_slot, k).wait_send()

    @pl.when(jnp.logical_not(stays))
    def _():
        final_copy(t, my_slot, 0).wait_send()


def write_kernel(logits, keys, values, logits_o, keys_o, values_o, sem):
    copies = [
        pltpu.make_async_copy(source, target, sem.at[i])
        for i, (source, target) in enumerate(
            ((logits, logits_o), (keys, keys_o), (values, values_o))
        )
    ]
    for copy in copies:
        copy.start()
    for copy in copies:
        copy.wait()


def local_kernel(
    n,
    nb,
    hidden,
    w_qkv,
    key_cache,
    value_cache,
    lengths,
    w_out,
    router,
    routes,
    w_gate,
    w_up,
    w_down,
    w_vocab,
    group_ids,
    weight_index,
    guidance_levels,
):
    count, width = hidden.shape[1:]
    span, kv_width = key_cache.shape[2:]
    cols = width // n
    units = w_gate.shape[1]
    vocab = w_vocab.shape[1]
    half = nb // 2
    kept = half * count
    vmem = pl.BlockSpec(memory_space=pltpu.VMEM)
    smem = pl.BlockSpec(memory_space=pltpu.SMEM)
    anywhere = pl.BlockSpec(memory_space=pl.ANY)
    in_hbm = pl.BlockSpec(memory_space=pltpu.HBM)
    packed = cols + 2 * LANES
    chunk = pltpu.VMEM((n, count, cols), BF16)
    tiles, vocab_tiles = units // TILE, vocab // TILE
    weights = 2 * (3 * width * units + width * vocab + w_qkv.size + w_out.size)
    results = pl.pallas_call(
        functools.partial(step_kernel, n, nb),
        out_shape=(
            jax.ShapeDtypeStruct((kept, vocab), F32),
            jax.ShapeDtypeStruct((1, count, kv_width), BF16),
            jax.ShapeDtypeStruct((1, count, kv_width), BF16),
        ),
        in_specs=[vmem, smem, vmem, smem, smem, smem, smem] + [anywhere] * 8,
        out_specs=(vmem, vmem, vmem),
        scratch_shapes=[
            pltpu.VMEM(w_qkv.shape, BF16),
            pltpu.VMEM(key_cache.shape[1:], BF16),
            pltpu.VMEM(value_cache.shape[1:], BF16),
            pltpu.VMEM(w_out.shape, BF16),
            pltpu.VMEM((tiles, width, TILE), BF16),
            pltpu.VMEM((tiles, width, TILE), BF16),
            pltpu.VMEM((tiles, TILE, width), BF16),
            pltpu.VMEM((vocab_tiles, width, TILE), BF16),
            pltpu.VMEM((n, count, packed), F32),
            pltpu.VMEM((n, count, packed), F32),
            pltpu.VMEM((n, count, packed), BF16),
            chunk,
            chunk,
            pltpu.VMEM((n, count, LANES), F32),
            chunk,
            chunk,
            chunk,
            chunk,
            chunk,
            chunk,
            pltpu.VMEM((count, width), BF16),
            pltpu.VMEM((2 * half, count, width), BF16),
            pltpu.SemaphoreType.DMA((4,)),
            pltpu.SemaphoreType.DMA((4, max(tiles, vocab_tiles))),
            pltpu.SemaphoreType.DMA((PHASES, n)),
            pltpu.SemaphoreType.DMA((PHASES, n)),
            pltpu.SemaphoreType.DMA((nb,)),
            pltpu.SemaphoreType.DMA((2 * half,)),
        ],
        compiler_params=pltpu.CompilerParams(
            collective_id=0, has_side_effects=True, vmem_limit_bytes=60 * 2**20
        ),
        cost_estimate=pl.CostEstimate(
            flops=weights * count, bytes_accessed=weights, transcendentals=count * units
        ),
    )(
        hidden,
        lengths,
        router.T,
        jnp.swapaxes(routes, 1, 2),
        group_ids,
        weight_index,
        guidance_levels,
        w_qkv,
        key_cache,
        value_cache,
        w_out,
        w_gate,
        w_up,
        w_down,
        w_vocab,
    )
    return pl.pallas_call(
        write_kernel,
        out_shape=tuple(jax.ShapeDtypeStruct(part.shape, part.dtype) for part in results),
        in_specs=[in_hbm] * 3,
        out_specs=(in_hbm,) * 3,
        scratch_shapes=[pltpu.SemaphoreType.DMA((3,))],
        compiler_params=pltpu.CompilerParams(vmem_limit_bytes=60 * 2**20),
    )(*results)


def fits_kernel(mesh):
    return KV_HEADS * HEAD_DIM == mesh.shape["blk"] * LANES and mesh.shape["batch"] % 2 == 0


def solution(mesh):
    if fits_kernel(mesh):
        body = functools.partial(local_kernel, mesh.shape["blk"], mesh.shape["batch"])
    else:
        body = local
    placed = (
        P("guide", "batch", None),
        P("blk", None),
        P("guide", "batch", "blk", None),
        P("guide", "batch", "blk", None),
        P("guide", "batch"),
        P("blk", None),
        P(),
        P("guide", "batch", None),
        P(None, "blk"),
        P(None, "blk"),
        P("blk", None),
        P(None, ("blk", "batch")),
        P(),
        P(),
        P(),
    )
    return jax.shard_map(
        body,
        mesh=mesh,
        in_specs=placed,
        out_specs=(
            P("guide", ("blk", "batch")),
            P("guide", "batch", None),
            P("guide", "batch", None),
        ),
        check_vma=False,
    )
```

```python
import functools

import jax
import jax.numpy as jnp
from jax import lax
from jax.experimental import pallas as pl
from jax.experimental.pallas import tpu as pltpu
from jax.sharding import PartitionSpec as P

HEADS = 24
KV_HEADS = 8
HEAD_DIM = 64
EXPERTS = 16
EXPERT_UNITS = 1024


EPS = 1e-05


def from_partner(value, axis, bit):
    mask = 2**bit
    pairs = [(source, source ^ mask) for source in range(lax.axis_size(axis))]
    return lax.ppermute(value, axis, pairs)


def rms(values):
    return values * lax.rsqrt(jnp.mean(values * values, axis=-1, keepdims=True) + EPS)


def local(
    hidden,
    w_qkv,
    key_cache,
    value_cache,
    lengths,
    w_out,
    router,
    routes,
    w_gate,
    w_up,
    w_down,
    w_vocab,
    group_ids,
    weight_index,
    guidance_levels,
):
    width_q = HEADS * HEAD_DIM
    width_k = KV_HEADS * HEAD_DIM
    group = HEADS // KV_HEADS
    position_block = lax.axis_index("blk")
    count = hidden.shape[1]
    x = hidden[0].astype(jnp.float32)
    normed = rms(x).astype(jnp.bfloat16)
    feat_rows = w_qkv.shape[0]
    normed_part = lax.dynamic_slice_in_dim(normed, position_block * feat_rows, feat_rows, 1)
    partial_qkv = jnp.dot(normed_part, w_qkv, preferred_element_type=jnp.float32)
    qkv = lax.psum(partial_qkv, "blk").astype(jnp.bfloat16)
    query = qkv[:, :width_q]
    new_key = qkv[:, width_q : width_q + width_k]
    new_value = qkv[:, width_q + width_k :]
    span = key_cache.shape[2]
    query_heads = query.reshape(count, KV_HEADS, group, HEAD_DIM)
    keys_here = key_cache[0].reshape(count, span, KV_HEADS, HEAD_DIM)
    values_here = value_cache[0].reshape(count, span, KV_HEADS, HEAD_DIM)
    scale = HEAD_DIM ** (-0.5)
    scores = (
        jnp.einsum("rkgd,rckd->rkgc", query_heads, keys_here, preferred_element_type=jnp.float32)
        * scale
    )
    own = (
        jnp.einsum(
            "rkgd,rkd->rkg",
            query_heads,
            new_key.reshape(count, KV_HEADS, HEAD_DIM),
            preferred_element_type=jnp.float32,
        )
        * scale
    )
    positions = position_block * span + jnp.arange(span)
    valid = (positions[None, :] < lengths[0][:, None])[:, None, None, :]
    local_top = jnp.max(jnp.where(valid, scores, -1e30), axis=-1)
    top = lax.pmax(jnp.maximum(local_top, own), "blk")
    probs = jnp.exp(jnp.where(valid, scores - top[..., None], -1e30))
    partial_total = jnp.sum(probs, axis=-1)
    acc = jnp.einsum(
        "rkgc,rckd->rkgd",
        probs.astype(jnp.bfloat16),
        values_here,
        preferred_element_type=jnp.float32,
    ).reshape(count, width_q)
    own_prob = jnp.exp(own - top)
    own_rounded = lax.optimization_barrier(own_prob.astype(jnp.bfloat16)).astype(jnp.float32)
    own_term = (
        own_rounded[..., None] * new_value.astype(jnp.float32).reshape(count, KV_HEADS, 1, HEAD_DIM)
    ).reshape(count, width_q)
    out_rows = w_out.shape[0]
    acc_sum, total_sum = lax.psum((acc, partial_total), "blk")
    totals = jnp.repeat((total_sum + own_prob).reshape(count, HEADS), HEAD_DIM, axis=1)
    attn = ((acc_sum + own_term) / totals).astype(jnp.bfloat16)
    attn_cols = lax.dynamic_slice_in_dim(attn, position_block * out_rows, out_rows, 1)
    mixed = x + lax.psum(jnp.dot(attn_cols, w_out, preferred_element_type=jnp.float32), "blk")
    expert_in = rms(mixed).astype(jnp.bfloat16)
    choice_logits = jnp.dot(expert_in, router, preferred_element_type=jnp.float32)
    picks = (routes[0][:, :, None] == jnp.arange(EXPERTS)[None, None, :]).astype(jnp.float32)
    chosen = jnp.sum(picks * choice_logits[:, None, :], axis=-1)
    first = jax.nn.sigmoid(chosen[:, 0] - chosen[:, 1])
    shares = jnp.stack([first, 1.0 - first], axis=1)
    per_expert = jnp.sum(picks * shares[:, :, None], axis=1)
    local_units = w_gate.shape[1]
    owner = (position_block * local_units + jnp.arange(local_units)) // EXPERT_UNITS
    member = (owner[None, :] == jnp.arange(EXPERTS)[:, None]).astype(jnp.float32)
    unit_weight = jnp.sum(per_expert[:, :, None] * member[None, :, :], axis=1)
    gate = jnp.dot(expert_in, w_gate, preferred_element_type=jnp.float32)
    upper = jnp.dot(expert_in, w_up, preferred_element_type=jnp.float32)
    act = (jax.nn.silu(gate) * upper * unit_weight).astype(jnp.bfloat16)
    expert_out = lax.psum(jnp.dot(act, w_down, preferred_element_type=jnp.float32), "blk")
    final_in = rms(mixed + expert_out).astype(jnp.bfloat16)
    stream_logits = jnp.dot(
        lax.all_gather(final_in, "batch", axis=0, tiled=True),
        w_vocab,
        preferred_element_type=jnp.float32,
    ).astype(jnp.bfloat16)
    stream_index = lax.axis_index("guide")
    half_rows = stream_logits.shape[0] // 2
    kept_rows = lax.dynamic_slice_in_dim(stream_logits, stream_index * half_rows, half_rows, 0)
    sent_rows = lax.dynamic_slice_in_dim(
        stream_logits, (1 - stream_index) * half_rows, half_rows, 0
    )
    partner = from_partner(sent_rows, "guide", 0)
    is_first = stream_index == 0
    cond = jnp.where(is_first, kept_rows, partner).astype(jnp.float32)
    uncond = jnp.where(is_first, partner, kept_rows).astype(jnp.float32)
    group_count = weight_index.shape[0]
    level_count = guidance_levels.shape[0]
    in_group = (group_ids[:, None] == jnp.arange(group_count)[None, :]).astype(jnp.float32)
    level_pick = (weight_index[:, None] == jnp.arange(level_count)[None, :]).astype(jnp.float32)
    group_weight = jnp.sum(level_pick * guidance_levels[None, :], axis=1)
    request_weight = jnp.sum(in_group * group_weight[None, :], axis=1)
    weight_rows = lax.dynamic_slice_in_dim(request_weight, stream_index * half_rows, half_rows, 0)
    logits = uncond + weight_rows[:, None] * (cond - uncond)
    return (logits, new_key[None], new_value[None])


TILE = 512
LANES = 128
MESH = pl.DeviceIdType.MESH
F32 = jnp.float32
BF16 = jnp.bfloat16
HIGH = lax.Precision.HIGHEST
PHASES = 8
QKV_SUM, QKV_ALL, ATT_SUM, ATT_STAT, OUT_SUM, MIX_ALL, EXP_SUM, FIN_ALL = range(PHASES)


def iota(shape, dim):
    return lax.broadcasted_iota(jnp.int32, shape, dim)


def step_kernel(
    n,
    nb,
    hidden,
    lengths,
    router,
    routes,
    group_ids,
    weight_index,
    levels,
    w_qkv,
    key_cache,
    value_cache,
    w_out,
    w_gate,
    w_up,
    w_down,
    w_vocab,
    logits_o,
    keys_o,
    values_o,
    qkv_v,
    key_v,
    value_v,
    out_v,
    gate_v,
    up_v,
    down_v,
    vocab_v,
    qkv_part,
    qkv_sum,
    qkv_all,
    att_part,
    att_sum,
    att_stat,
    out_part,
    out_sum,
    mix_all,
    exp_part,
    exp_sum,
    fin_all,
    final_own,
    final_all,
    load_sem,
    tile_sem,
    send_sem,
    recv_sem,
    fin_send,
    fin_recv,
):
    g = lax.axis_index("guide")
    b = lax.axis_index("blk")
    t = lax.axis_index("batch")
    half = nb // 2
    count, width = hidden.shape[1:]
    span = key_cache.shape[2]
    cols = width // n
    kv_width = key_cache.shape[3]
    group = HEADS // KV_HEADS
    tiles = gate_v.shape[0]
    vocab_tiles = vocab_v.shape[0]
    my_cols = pl.ds(pl.multiple_of(b * cols, LANES), cols)

    loads = [
        pltpu.make_async_copy(w_qkv, qkv_v, load_sem.at[0]),
        pltpu.make_async_copy(key_cache.at[0], key_v, load_sem.at[1]),
        pltpu.make_async_copy(value_cache.at[0], value_v, load_sem.at[2]),
        pltpu.make_async_copy(w_out, out_v, load_sem.at[3]),
    ]
    for load in loads:
        load.start()

    barrier = pltpu.get_barrier_semaphore()
    for k in range(1, n):
        pl.semaphore_signal(
            barrier, inc=1, device_id={"blk": lax.rem(b + k, n)}, device_id_type=MESH
        )
    for k in range(1, 2 * nb):
        other = lax.rem(g * nb + t + k, 2 * nb)
        pl.semaphore_signal(
            barrier,
            inc=1,
            device_id={"guide": other // nb, "batch": lax.rem(other, nb)},
            device_id_type=MESH,
        )

    def tile_cols(i):
        return pl.ds(pl.multiple_of(i * TILE, TILE), TILE)

    def gate_load(i):
        return pltpu.make_async_copy(w_gate.at[:, tile_cols(i)], gate_v.at[i], tile_sem.at[0, i])

    def up_load(i):
        return pltpu.make_async_copy(w_up.at[:, tile_cols(i)], up_v.at[i], tile_sem.at[1, i])

    def down_load(i):
        return pltpu.make_async_copy(w_down.at[tile_cols(i), :], down_v.at[i], tile_sem.at[2, i])

    def vocab_load(i):
        return pltpu.make_async_copy(w_vocab.at[:, tile_cols(i)], vocab_v.at[i], tile_sem.at[3, i])

    def send(phase, source, landing):
        for k in range(1, n):
            peer = lax.rem(b + k, n)
            pltpu.make_async_remote_copy(
                src_ref=source(peer),
                dst_ref=landing.at[b],
                send_sem=send_sem.at[phase, k - 1],
                recv_sem=recv_sem.at[phase, b],
                device_id={"blk": peer},
                device_id_type=MESH,
            ).start()

    def arrive(phase, landing):
        for k in range(1, n):
            peer = lax.rem(b + k, n)
            pltpu.make_async_remote_copy(
                src_ref=landing.at[peer],
                dst_ref=landing.at[peer],
                send_sem=send_sem.at[phase, k - 1],
                recv_sem=recv_sem.at[phase, peer],
                device_id={"blk": peer},
                device_id_type=MESH,
            ).wait_recv()

    def drain(phase, landing):
        for k in range(1, n):
            peer = lax.rem(b + k, n)
            pltpu.make_async_remote_copy(
                src_ref=landing.at[b],
                dst_ref=landing.at[b],
                send_sem=send_sem.at[phase, k - 1],
                recv_sem=recv_sem.at[phase, b],
                device_id={"blk": peer},
                device_id_type=MESH,
            ).wait_send()

    def summed(landing):
        total = landing[0].astype(F32)
        for j in range(1, n):
            total = total + landing[j].astype(F32)
        return total

    def joined(landing):
        return jnp.concatenate([landing[j] for j in range(n)], axis=1)

    def inverse_rms(values):
        return lax.rsqrt(jnp.mean(values * values, axis=-1, keepdims=True) + EPS)

    inverse = inverse_rms(hidden[0].astype(F32))
    normed = (hidden[0, :, my_cols].astype(F32) * inverse).astype(BF16)
    loads[0].wait()

    def start_expert(i, carry):
        gate_load(i).start()
        up_load(i).start()
        down_load(i).start()
        return carry

    def start_vocab(i, carry):
        vocab_load(i).start()
        return carry

    for j in range(n):
        starts = (
            (0, cols, j * cols),
            (cols, LANES, width + j * LANES),
            (cols + LANES, LANES, width + kv_width + j * LANES),
        )
        for at, size, begin in starts:
            qkv_part[j, :, at : at + size] = jnp.dot(
                normed, qkv_v[:, begin : begin + size], preferred_element_type=F32
            )
    qkv_sum[b] = qkv_part[b]
    pl.semaphore_wait(barrier, n - 1 + 2 * nb - 1)
    send(QKV_SUM, lambda peer: qkv_part.at[peer], qkv_sum)
    lax.fori_loop(0, tiles, start_expert, 0)
    lax.fori_loop(0, vocab_tiles, start_vocab, 0)

    kept = final_all.shape[0] // 2 * count
    row = iota((kept, 1), 0)

    def pick_weight(i, column):
        level = levels[weight_index[group_ids[g * kept + i]]]
        return jnp.where(row == i, level, column)

    weight = lax.fori_loop(0, kept, pick_weight, jnp.zeros((kept, 1), F32))

    request = iota((count, 1), 0)
    chosen_first = jnp.zeros((count, 1), jnp.int32)
    chosen_second = jnp.zeros((count, 1), jnp.int32)
    for r in range(count):
        chosen_first = jnp.where(request == r, routes[0, 0, r], chosen_first)
        chosen_second = jnp.where(request == r, routes[0, 1, r], chosen_second)

    low = iota((count, LANES), 1) < HEAD_DIM
    arrive(QKV_SUM, qkv_sum)
    total = summed(qkv_sum)
    va, vb, vc, vk, vv = (total[:, LANES * i : LANES * (i + 1)] for i in range(5))
    q0 = jnp.where(low, va, vb).astype(BF16)
    q1 = jnp.where(low, pltpu.roll(va, HEAD_DIM, 1), pltpu.roll(vc, HEAD_DIM, 1)).astype(BF16)
    q2 = jnp.where(low, vb, vc).astype(BF16)
    own_key = vk.astype(BF16)
    own_value = vv.astype(BF16)
    qkv_all[b] = jnp.concatenate([q0, q1, q2, own_key, own_value], axis=1)
    send(QKV_ALL, lambda peer: qkv_all.at[b], qkv_all)

    scale = HEAD_DIM ** (-0.5)
    same_head = (
        iota((LANES, LANES), 0) // HEAD_DIM == iota((LANES, LANES), 1) // HEAD_DIM
    ).astype(F32)
    own_score = jnp.concatenate(
        [
            jnp.dot(
                q.astype(F32) * own_key.astype(F32),
                same_head,
                precision=HIGH,
                preferred_element_type=F32,
            )
            for q in (q0, q1, q2)
        ],
        axis=1,
    ) * scale
    own_value3 = jnp.concatenate([own_value.astype(F32)] * group, axis=1)
    heads = group * KV_HEADS
    rows = count * heads
    places = count * span
    place = iota((1, places), 1)
    limit = jnp.zeros((1, places), jnp.int32)
    for r in range(count):
        limit = jnp.where(place // span == r, lengths[0, r], limit)
    in_cache = b * span + lax.rem(place, span) < limit
    valid = jnp.logical_and(iota((rows, 1), 0) // heads == place // span, in_cache)
    head_lanes = (
        iota((KV_HEADS, kv_width), 1) // HEAD_DIM == iota((KV_HEADS, kv_width), 0)
    ).astype(F32)[None]
    loads[1].wait()
    loads[2].wait()

    arrive(QKV_ALL, qkv_all)
    for j in range(n):
        spot = slice(LANES * j, LANES * (j + 1))
        keys_o[0, :, spot] = qkv_all[j, :, cols : cols + LANES]
        values_o[0, :, spot] = qkv_all[j, :, cols + LANES : cols + 2 * LANES]
    spread = []
    for i in range(group):
        query = jnp.concatenate(
            [qkv_all[j, :, LANES * i : LANES * (i + 1)] for j in range(n)], axis=1
        )
        spread.append(query.astype(F32)[:, None, :] * head_lanes)
    spread = jnp.concatenate(spread, axis=1).reshape(rows, kv_width).astype(BF16)
    scores = (
        lax.dot_general(
            spread,
            key_v[...].reshape(places, kv_width),
            (((1,), (1,)), ((), ())),
            preferred_element_type=F32,
        )
        * scale
    )
    top = jnp.max(jnp.where(valid, scores, -1e30), axis=1, keepdims=True)
    probs = jnp.exp(jnp.where(valid, scores - top, -1e30))
    mass = jnp.sum(probs, axis=1, keepdims=True)
    acc = jnp.dot(
        probs.astype(BF16), value_v[...].reshape(places, kv_width), preferred_element_type=F32
    ).reshape(count, heads, kv_width)
    for i in range(group):
        mine = jnp.sum(acc[:, KV_HEADS * i : KV_HEADS * (i + 1), :] * head_lanes, axis=1)
        for j in range(n):
            att_part[j, :, LANES * i : LANES * (i + 1)] = mine[
                :, LANES * j : LANES * (j + 1)
            ].astype(BF16)
    lane = iota((heads, LANES), 1)
    slot = iota((heads, LANES), 0)
    packed = jnp.where(lane[None] == slot[None], top.reshape(count, heads, 1), 0.0) + jnp.where(
        lane[None] == slot[None] + HEAD_DIM, mass.reshape(count, heads, 1), 0.0
    )
    att_stat[b] = jnp.sum(packed, axis=1)
    att_sum[b] = att_part[b]
    send(ATT_STAT, lambda peer: att_stat.at[b], att_stat)
    send(ATT_SUM, lambda peer: att_part.at[peer], att_sum)

    from_lane = iota((LANES, cols), 0)
    to_lane = iota((LANES, cols), 1)
    head_of = (
        to_lane // LANES * KV_HEADS
        + b * (KV_HEADS // n)
        + lax.rem(to_lane, LANES) // HEAD_DIM
    )
    pick_top = (from_lane == head_of).astype(F32)
    pick_mass = (from_lane == head_of + HEAD_DIM).astype(F32)
    loads[3].wait()
    arrive(ATT_STAT, att_stat)
    stats = att_stat[...].reshape(n * count, LANES)
    tops = jnp.dot(stats, pick_top, precision=HIGH, preferred_element_type=F32)
    masses = jnp.dot(stats, pick_mass, precision=HIGH, preferred_element_type=F32)
    best = own_score
    for j in range(n):
        best = jnp.maximum(best, tops[count * j : count * (j + 1)])
    own_prob = jnp.exp(own_score - best)
    denominator = own_prob
    numerator = own_prob.astype(BF16).astype(F32) * own_value3
    arrive(ATT_SUM, att_sum)
    for j in range(n):
        share = jnp.exp(tops[count * j : count * (j + 1)] - best)
        denominator = denominator + share * masses[count * j : count * (j + 1)]
        numerator = numerator + share * att_sum[j].astype(F32)
    a0, a1, a2 = (
        (numerator / denominator)[:, LANES * i : LANES * (i + 1)] for i in range(group)
    )
    turned = pltpu.roll(a1, HEAD_DIM, 1)
    attn = jnp.concatenate(
        [jnp.where(low, a0, turned), jnp.where(low, a2, a0), jnp.where(low, turned, a2)], axis=1
    ).astype(BF16)
    for j in range(n):
        out_part[j] = jnp.dot(
            attn, out_v[:, cols * j : cols * (j + 1)], preferred_element_type=F32
        ).astype(BF16)
    out_sum[b] = out_part[b]
    send(OUT_SUM, lambda peer: out_part.at[peer], out_sum)
    arrive(OUT_SUM, out_sum)
    mixed = hidden[0, :, my_cols].astype(F32) + summed(out_sum)
    mix_all[b] = mixed.astype(BF16)
    send(MIX_ALL, lambda peer: mix_all.at[b], mix_all)
    arrive(MIX_ALL, mix_all)

    expert_in = joined(mix_all)
    inverse = inverse_rms(expert_in.astype(F32))
    choice = (
        lax.dot_general(
            expert_in, router[...], (((1,), (1,)), ((), ())), preferred_element_type=F32
        )
        * inverse
    )
    expert = iota((count, EXPERTS), 1)
    is_first = (expert == chosen_first).astype(F32)
    is_second = (expert == chosen_second).astype(F32)
    gap = jnp.sum((is_first - is_second) * choice, axis=1, keepdims=True)
    first = 1.0 / (1.0 + jnp.exp(-gap))
    per_expert = is_first * first + is_second * (1.0 - first)

    def expert_tile(i, out):
        gate_load(i).wait()
        gate = jnp.dot(expert_in, gate_v[i], preferred_element_type=F32) * inverse
        up_load(i).wait()
        upper = jnp.dot(expert_in, up_v[i], preferred_element_type=F32) * inverse
        owner = (b * tiles + i) * TILE // EXPERT_UNITS
        share = jnp.sum(jnp.where(expert == owner, per_expert, 0.0), axis=1, keepdims=True)
        act = (gate / (1.0 + jnp.exp(-gate)) * upper * share).astype(BF16)
        down_load(i).wait()
        return out + jnp.dot(act, down_v[i], preferred_element_type=F32)

    expert_out = lax.fori_loop(0, tiles, expert_tile, jnp.zeros((count, width), F32))
    for j in range(n):
        exp_part[j] = expert_out[:, cols * j : cols * (j + 1)].astype(BF16)
    exp_sum[b] = exp_part[b]
    send(EXP_SUM, lambda peer: exp_part.at[peer], exp_sum)
    arrive(EXP_SUM, exp_sum)
    fin_all[b] = (mixed + summed(exp_sum)).astype(BF16)
    send(FIN_ALL, lambda peer: fin_all.at[b], fin_all)
    arrive(FIN_ALL, fin_all)
    final_own[...] = joined(fin_all)

    def final_copy(to_batch, landing_slot, send_slot):
        return pltpu.make_async_remote_copy(
            src_ref=final_own,
            dst_ref=final_all.at[landing_slot],
            send_sem=fin_send.at[send_slot],
            recv_sem=fin_recv.at[landing_slot],
            device_id={"guide": t // half, "batch": to_batch},
            device_id_type=MESH,
        )

    my_slot = g * half + lax.rem(t, half)
    stays = g == t // half
    for k in range(1, nb):
        final_copy(lax.rem(t + k, nb), my_slot, k).start()

    @pl.when(stays)
    def _():
        final_all[my_slot] = final_own[...]

    @pl.when(jnp.logical_not(stays))
    def _():
        final_copy(t, my_slot, 0).start()

    for s in range(2):
        for j in range(half):
            from_me = jnp.logical_and(g == s, t == g * half + j)

            @pl.when(jnp.logical_not(from_me))
            def _():
                final_copy(t, s * half + j, 0).wait_recv()

    finals = final_all[...].reshape(2 * half * count, width)
    inverse = inverse_rms(finals.astype(F32))

    def vocab_tile(i, carry):
        vocab_load(i).wait()
        streams = jnp.dot(finals, vocab_v[i], preferred_element_type=F32) * inverse
        cond, uncond = streams[:kept], streams[kept:]
        logits_o[:, tile_cols(i)] = uncond + weight * (cond - uncond)
        return carry

    lax.fori_loop(0, vocab_tiles, vocab_tile, 0)

    for phase, landing in (
        (QKV_SUM, qkv_sum),
        (QKV_ALL, qkv_all),
        (ATT_SUM, att_sum),
        (ATT_STAT, att_stat),
        (OUT_SUM, out_sum),
        (MIX_ALL, mix_all),
        (EXP_SUM, exp_sum),
        (FIN_ALL, fin_all),
    ):
        drain(phase, landing)
    for k in range(1, nb):
        final_copy(lax.rem(t + k, nb), my_slot, k).wait_send()

    @pl.when(jnp.logical_not(stays))
    def _():
        final_copy(t, my_slot, 0).wait_send()


def write_kernel(logits, keys, values, logits_o, keys_o, values_o):
    logits_o[...] = logits[...]
    keys_o[...] = keys[...]
    values_o[...] = values[...]


def local_kernel(
    n,
    nb,
    hidden,
    w_qkv,
    key_cache,
    value_cache,
    lengths,
    w_out,
    router,
    routes,
    w_gate,
    w_up,
    w_down,
    w_vocab,
    group_ids,
    weight_index,
    guidance_levels,
):
    count, width = hidden.shape[1:]
    span, kv_width = key_cache.shape[2:]
    cols = width // n
    units = w_gate.shape[1]
    vocab = w_vocab.shape[1]
    half = nb // 2
    kept = half * count
    vmem = pl.BlockSpec(memory_space=pltpu.VMEM)
    smem = pl.BlockSpec(memory_space=pltpu.SMEM)
    anywhere = pl.BlockSpec(memory_space=pl.ANY)
    packed = cols + 2 * LANES
    chunk = pltpu.VMEM((n, count, cols), BF16)
    tiles, vocab_tiles = units // TILE, vocab // TILE
    weights = 2 * (3 * width * units + width * vocab + w_qkv.size + w_out.size)
    results = pl.pallas_call(
        functools.partial(step_kernel, n, nb),
        out_shape=(
            jax.ShapeDtypeStruct((kept, vocab), F32),
            jax.ShapeDtypeStruct((1, count, kv_width), BF16),
            jax.ShapeDtypeStruct((1, count, kv_width), BF16),
        ),
        in_specs=[vmem, smem, vmem, smem, smem, smem, smem] + [anywhere] * 8,
        out_specs=(vmem, vmem, vmem),
        scratch_shapes=[
            pltpu.VMEM(w_qkv.shape, BF16),
            pltpu.VMEM(key_cache.shape[1:], BF16),
            pltpu.VMEM(value_cache.shape[1:], BF16),
            pltpu.VMEM(w_out.shape, BF16),
            pltpu.VMEM((tiles, width, TILE), BF16),
            pltpu.VMEM((tiles, width, TILE), BF16),
            pltpu.VMEM((tiles, TILE, width), BF16),
            pltpu.VMEM((vocab_tiles, width, TILE), BF16),
            pltpu.VMEM((n, count, packed), F32),
            pltpu.VMEM((n, count, packed), F32),
            pltpu.VMEM((n, count, packed), BF16),
            chunk,
            chunk,
            pltpu.VMEM((n, count, LANES), F32),
            chunk,
            chunk,
            chunk,
            chunk,
            chunk,
            chunk,
            pltpu.VMEM((count, width), BF16),
            pltpu.VMEM((2 * half, count, width), BF16),
            pltpu.SemaphoreType.DMA((4,)),
            pltpu.SemaphoreType.DMA((4, max(tiles, vocab_tiles))),
            pltpu.SemaphoreType.DMA((PHASES, n)),
            pltpu.SemaphoreType.DMA((PHASES, n)),
            pltpu.SemaphoreType.DMA((nb,)),
            pltpu.SemaphoreType.DMA((2 * half,)),
        ],
        compiler_params=pltpu.CompilerParams(
            collective_id=0, has_side_effects=True, vmem_limit_bytes=60 * 2**20
        ),
        cost_estimate=pl.CostEstimate(
            flops=weights * count, bytes_accessed=weights, transcendentals=count * units
        ),
    )(
        hidden,
        lengths,
        router.T,
        jnp.swapaxes(routes, 1, 2),
        group_ids,
        weight_index,
        guidance_levels,
        w_qkv,
        key_cache,
        value_cache,
        w_out,
        w_gate,
        w_up,
        w_down,
        w_vocab,
    )
    return pl.pallas_call(
        write_kernel,
        out_shape=tuple(jax.ShapeDtypeStruct(part.shape, part.dtype) for part in results),
        in_specs=[vmem] * 3,
        out_specs=(vmem,) * 3,
    )(*results)


def fits_kernel(mesh):
    return KV_HEADS * HEAD_DIM == mesh.shape["blk"] * LANES and mesh.shape["batch"] % 2 == 0


def solution(mesh):
    if fits_kernel(mesh):
        body = functools.partial(local_kernel, mesh.shape["blk"], mesh.shape["batch"])
    else:
        body = local
    placed = (
        P("guide", "batch", None),
        P("blk", None),
        P("guide", "batch", "blk", None),
        P("guide", "batch", "blk", None),
        P("guide", "batch"),
        P("blk", None),
        P(),
        P("guide", "batch", None),
        P(None, "blk"),
        P(None, "blk"),
        P("blk", None),
        P(None, ("blk", "batch")),
        P(),
        P(),
        P(),
    )
    return jax.shard_map(
        body,
        mesh=mesh,
        in_specs=placed,
        out_specs=(
            P("guide", ("blk", "batch")),
            P("guide", "batch", None),
            P("guide", "batch", None),
        ),
        check_vma=False,
    )
```
